32 devices in a mesh: groups: 2 (over y), seq: 4 (over z), ep: 2 (over x), tp: 2 (over core).
Axes of the slice: x: 2, y: 2, z: 4, core: 2. Of those that a mesh axis runs over, the one named last changes fastest.
Arguments:
- hidden: bfloat16 [2048, 1440], P(('groups', 'seq', 'ep')), parts along dimension 0, may hold values from -6 to 6
- expert_ids: int32 [2048, 4], P(('groups', 'seq', 'ep')), parts along dimension 0, may hold values from 0 to 7, all different within a row; in each aligned block of 128 rows (0 to 127, 128 to 255, ...) at most 88 rows name the same one
- gate_units: int32 [2048, 4], P(('groups', 'seq', 'ep')), parts along dimension 0, may hold values from 4096 to 32767
- w_gate: bfloat16 [8, 1440, 1440], P(('seq', 'tp'), None, 'ep'), may hold values from -0.15625 to 0.15625
- w_up: bfloat16 [8, 1440, 1440], P(('seq', 'tp'), None, 'ep'), may hold values from -0.15625 to 0.15625
- w_down: bfloat16 [8, 1440, 1440], P(('seq', 'tp'), None, 'ep'), may hold values from -0.15625 to 0.15625
Outputs:
- moe_out: bfloat16 [2048, 1440], P(('groups', 'seq', 'ep'), 'tp'), parts along dimension 0
The draws below stay inside these ranges and needn't reach their ends.
There are 2 independent parts, one for each index of `groups`. The reference program is written for one: setup_inputs(seed, part) draws one part's arguments, and reference() takes and returns one part's arrays. A program takes and returns all parts, laid end to end along the dimension named above; an argument that names none is the same for every part. Nothing has to cross between parts.
Inputs may be any that keep to these rules, and one draw needn't show every extreme that they name: `expert_ids`: each row names 4 different experts; in each aligned block of 128 rows no expert is named by more than 88 rows, and in every draw some expert is named by exactly 88 rows of some block.
All inputs are finite; a program needn't handle non-finite values.
Results may differ from the reference program's by a relative error of at most 0.0064.
Values may be sent and summed in bfloat16 or wider, within the bound.
No kernel may reach another device: no remote copies, remote signals or barrier semaphores. Data moves between devices by JAX's collectives and lax.ppermute only.
A program may use at most 64 MiB of HBM per device.

```python
import math
import jax
import jax.numpy as jnp
import numpy as np
from jax import lax

D = 1440
FF = 1440
TOP = 4
TOK_DEV = 128
DOCUMENT_TOKENS = 1024
EXPERTS = 8
CAP = 88
N_EP = 2


def plant(result, key, least, largest):
    longest = result.shape.index(max(result.shape))
    spots = []
    for shift in (0, 1):
        where = [jax.random.randint(jax.random.fold_in(key, axis), (), 0, length) for axis, length in enumerate(result.shape)]
        where[longest] = (where[longest] + shift) % result.shape[longest]
        spots.append(tuple(where))
    return result.at[spots[0]].set(least).at[spots[1]].set(largest)


def levels(key, shape, shards, smallest, top_value):
    loudness = 1.0
    for position, shards_of in shards:
        draws = jax.random.uniform(jax.random.fold_in(jax.random.fold_in(key, 6), position), (shards_of,), jnp.float32, smallest / len(shards), top_value / len(shards))
        loudness = loudness * jnp.repeat(jnp.exp(draws), shape[position] // shards_of).reshape((-1,) + (1,) * (len(shape) - 1 - position))
    return loudness


def assign_block(key, own, number, rows, amount, top, limit, slope):
    order = jax.random.permutation(key, amount)
    crowded, ordinary = load_shares(amount, rows * top, limit, slope, True), load_shares(amount, rows * top, limit, slope, False)
    places = jnp.arange(amount)

    def named(sizes, rotation):
        used = int((sizes > 0).sum())
        fixed = max(1, used // 4)
        shifted = fixed + (places - fixed + rotation * (used - fixed)) % max(1, amount - fixed)
        return jnp.zeros((amount,), jnp.int32).at[order[jnp.where(places < fixed, places, shifted)]].set(jnp.asarray(sizes, jnp.int32))

    sizes = jnp.where(number % 4 == 0, named(crowded, number // 4), named(ordinary, number - number // 4 - 1))
    mixed = jax.random.permutation(jax.random.fold_in(own, 3), amount)
    giver, taker = mixed[0:amount // 2 * 2:2], mixed[1:amount // 2 * 2:2]
    room = jnp.minimum(sizes[giver] - 1, limit - sizes[taker]) // 2
    room = jnp.where((giver == order[0]) | (taker == order[0]) | (sizes[taker] == 0), 0, jnp.maximum(room, 0))
    shifted = jax.random.randint(jax.random.fold_in(own, 4), (amount // 2,), 0, 1 << 20) % (room + 1)
    sizes = sizes.at[giver].add(-shifted).at[taker].add(shifted)
    items = jnp.searchsorted(jnp.cumsum(sizes), jnp.arange(rows * top), side="right").astype(jnp.int32)
    listing = items.reshape(top, rows).T
    listing = listing[jax.random.permutation(jax.random.fold_in(own, 1), rows)]
    rotation = jax.random.randint(jax.random.fold_in(own, 2), (rows, 1), 0, top)
    return jnp.take_along_axis(listing, (jnp.arange(top)[None, :] + rotation) % top, axis=1)


def load_shares(amount, total, most, lean, full):
    portions = [(1 << 20) // math.isqrt(rank ** lean) + 1 for rank in range(1, amount + 1)]
    largest = most if full else min(most, max(-(-total // amount), total * portions[0] // sum(portions)))
    least = 1 if total - largest >= amount - 1 else 0
    counts, surplus = [largest] + [least] * (amount - 1), total - largest - least * (amount - 1)
    while surplus > 0:
        movable = [i for i in range(1, amount) if counts[i] < largest] or [i for i in range(1, amount) if counts[i] < most]
        whole, left = sum([portions[i] for i in movable]), surplus
        for i in movable:
            extra = min(most - counts[i], max(1, left * portions[i] // whole), surplus)
            counts[i] = counts[i] + extra
            surplus = surplus - extra
    return np.array(counts)


def bell_draw(stream_key, dims, scale, limit, cuts=(), kind=jnp.bfloat16):
    drawn = jax.random.normal(stream_key, dims, jnp.float32) * scale
    if len(cuts) > 0:
        drawn = levels(stream_key, dims, cuts, -0.22, 0.18) * drawn
    return jnp.clip(drawn, min=-limit, max=limit).astype(kind)


def setup_inputs(seed: int = 0, part: int = 0) -> dict:
    keys = jax.random.split(jax.random.key(seed), 7)
    part_keys = jax.random.split(jax.random.fold_in(keys[6], part), 7)
    hidden = bell_draw(part_keys[0], (DOCUMENT_TOKENS, D), 1.0, 6.0, ((0, 8),))
    expert_ids_keys = jax.random.split(jax.random.fold_in(part_keys[1], 1), DOCUMENT_TOKENS // TOK_DEV)
    expert_ids_turns = jax.random.permutation(jax.random.fold_in(part_keys[1], 3), DOCUMENT_TOKENS // TOK_DEV)
    expert_ids = jax.vmap(lambda own, number: assign_block(jax.random.fold_in(part_keys[1], 2), own, number, TOK_DEV, EXPERTS, TOP, CAP, 2))(expert_ids_keys, expert_ids_turns).reshape((DOCUMENT_TOKENS, TOP))
    gate_units = plant(jax.random.randint(part_keys[2], (DOCUMENT_TOKENS, TOP), 4096, 32768), jax.random.fold_in(part_keys[2], 1), 4096, 32767).astype(jnp.int32)
    w_gate = bell_draw(keys[3], (EXPERTS, D, FF), D ** -0.5, 0.15625, ((0, 8), (2, 2)))
    w_up = bell_draw(keys[4], (EXPERTS, D, FF), D ** -0.5, 0.15625, ((0, 8), (2, 2)))
    w_down = bell_draw(keys[5], (EXPERTS, D, FF), FF ** -0.5, 0.15625, ((0, 8), (2, 2)))
    return dict(hidden=hidden, expert_ids=expert_ids, gate_units=gate_units, w_gate=w_gate, w_up=w_up, w_down=w_down)


def expert_part(hidden, expert_ids, gate_units, w_gate, w_up, w_down):
    block_count = DOCUMENT_TOKENS // TOK_DEV
    pair_ids = expert_ids.reshape(block_count, TOK_DEV * TOP)
    onehot_ids = (pair_ids[:, :, None] == jnp.arange(EXPERTS, dtype=jnp.int32)[None, None, :]).astype(jnp.int32)
    slot_rank = jnp.sum((jnp.cumsum(onehot_ids, axis=1) - 1) * onehot_ids, axis=2).astype(jnp.int32)
    pair_index = jnp.arange(DOCUMENT_TOKENS * TOP, dtype=jnp.int32).reshape(block_count, TOK_DEV * TOP)
    block_index = jnp.broadcast_to(jnp.arange(block_count, dtype=jnp.int32)[:, None], pair_ids.shape)
    table = jnp.full((EXPERTS, block_count, CAP), -1, jnp.int32).at[pair_ids, block_index, slot_rank].set(pair_index)
    gate_share = gate_units.reshape(-1).astype(jnp.float32) / 65536.0
    slice_width = FF // N_EP

    def one_expert(running, expert):
        slots = table[expert].reshape(-1)
        live = slots >= 0
        safe = jnp.where(live, slots, 0).astype(jnp.int32)
        token_at = (safe // TOP).astype(jnp.int32)
        rows_in = hidden[token_at]
        gate_all = lax.dynamic_index_in_dim(w_gate, expert, 0, keepdims=False)
        up_all = lax.dynamic_index_in_dim(w_up, expert, 0, keepdims=False)
        down_all = lax.dynamic_index_in_dim(w_down, expert, 0, keepdims=False)
        summed = jnp.zeros((rows_in.shape[0], D), jnp.float32)
        for part_index in range(N_EP):
            lower = part_index * slice_width
            upper = lower + slice_width
            gate_pre = jnp.dot(rows_in, gate_all[:, lower:upper], preferred_element_type=jnp.float32)
            up_pre = jnp.dot(rows_in, up_all[:, lower:upper], preferred_element_type=jnp.float32)
            activation = ((up_pre + 1.0) * gate_pre * jax.nn.sigmoid(1.702 * gate_pre)).astype(jnp.bfloat16)
            slice_part = jnp.dot(activation, down_all[:, lower:upper].T, preferred_element_type=jnp.float32).astype(jnp.bfloat16)
            summed = summed + lax.optimization_barrier(slice_part).astype(jnp.float32)
        expert_out = summed.astype(jnp.bfloat16).astype(jnp.float32)
        weight = jnp.where(live, gate_share[safe], jnp.float32(0.0))
        running = running.at[token_at].add(weight[:, None] * expert_out)
        return running, None

    start_acc = jnp.zeros((DOCUMENT_TOKENS, D), jnp.float32)
    total, _ = lax.scan(one_expert, start_acc, jnp.arange(EXPERTS, dtype=jnp.int32))
    return total.astype(jnp.bfloat16)


def reference(hidden, expert_ids, gate_units, w_gate, w_up, w_down):
    return expert_part(hidden, expert_ids, gate_units, w_gate, w_up, w_down)
```

```python
import functools

import jax
import jax.numpy as jnp
from jax import lax
from jax.experimental import pallas as pl
from jax.experimental.pallas import tpu as pltpu
from jax.sharding import PartitionSpec as P

TOP = 4


def slice_output(rows_in, gate_cols, up_cols, down_cols):
    gate_pre = jnp.dot(rows_in, gate_cols, preferred_element_type=jnp.float32)
    up_pre = jnp.dot(rows_in, up_cols, preferred_element_type=jnp.float32)
    activation = ((up_pre + 1.0) * gate_pre * jax.nn.sigmoid(1.702 * gate_pre)).astype(jnp.bfloat16)
    return lax.dot_general(
        activation, down_cols, (((1,), (1,)), ((), ())), preferred_element_type=jnp.float32
    ).astype(jnp.bfloat16)


def capacity_of(token_count, expert_count):
    return max(2, (token_count * TOP * 11 + expert_count * 8 - 1) // (expert_count * 8))


def routed(hidden, expert_ids, gate_units, w_gate, w_up, w_down):
    token_count, model_width = hidden.shape
    seq_count = lax.axis_size("seq")
    ep_count = lax.axis_size("ep")
    tp_count = lax.axis_size("tp")
    half_width = model_width // tp_count
    my_half = lax.axis_index("tp")
    expert_count = seq_count * tp_count
    capacity = capacity_of(token_count, expert_count)
    flat_ids = expert_ids.reshape(-1)
    onehot_ids = (flat_ids[:, None] == jnp.arange(expert_count, dtype=jnp.int32)[None, :]).astype(
        jnp.int32
    )
    slot_rank = jnp.sum((jnp.cumsum(onehot_ids, axis=0) - 1) * onehot_ids, axis=1)
    owner_seq = flat_ids // tp_count
    owner_half = flat_ids % tp_count
    send_row = jnp.where(owner_half == my_half, owner_seq * capacity + slot_rank, -1)
    selector = jnp.arange(seq_count * capacity, dtype=jnp.int32)[:, None] == send_row[None, :]
    selector = jnp.any(selector.reshape(seq_count * capacity, token_count, TOP), axis=2).astype(
        jnp.bfloat16
    )
    outgoing = jnp.dot(selector, hidden, preferred_element_type=jnp.float32).astype(jnp.bfloat16)
    outgoing = outgoing.reshape(seq_count, capacity, model_width)
    column_of = (owner_half * seq_count + owner_seq) * capacity + slot_rank
    gate_share = gate_units.reshape(-1).astype(jnp.float32) / 65536.0
    column_ids = jnp.arange(tp_count * seq_count * capacity, dtype=jnp.int32)
    combiner = jnp.where(column_ids[None, :] == column_of[:, None], gate_share[:, None], 0.0)
    combiner = jnp.sum(combiner.reshape(token_count, TOP, -1), axis=1)
    copied = jnp.broadcast_to(outgoing[:, None], (seq_count, ep_count, capacity, model_width))
    copied = copied.reshape(seq_count * ep_count, capacity, model_width)
    arrived = lax.all_to_all(copied, ("seq", "ep"), split_axis=0, concat_axis=0, tiled=True)
    slice_rows = slice_output(arrived.reshape(-1, model_width), w_gate[0], w_up[0], w_down[0])
    slice_rows = slice_rows.reshape(seq_count * ep_count, capacity, model_width)
    came_back = lax.all_to_all(
        lax.all_to_all(slice_rows, ("seq", "ep"), split_axis=0, concat_axis=0, tiled=True),
        "tp",
        split_axis=2,
        concat_axis=0,
        tiled=True,
    )
    came_back = came_back.reshape(tp_count, seq_count, ep_count, capacity, half_width)
    returned = jnp.sum(came_back.astype(jnp.float32), axis=2).astype(jnp.bfloat16)
    result_rows = returned.reshape(-1, half_width).astype(jnp.float32)
    moe_out = jnp.dot(
        combiner, result_rows, precision=lax.Precision.HIGHEST, preferred_element_type=jnp.float32
    )
    return moe_out.astype(jnp.bfloat16)


def expert_kernel(
    expert_count, place_ref, a0, a1, b0, b1, wg, wu, wd, keep_a, keep_b, send, vg, vu, vd, rows, sems
):
    model_width, _ = wg.shape
    half_rows = a0.shape[0]
    half_width = model_width // 2
    tp, expert = place_ref[0], place_ref[1]
    copies = [
        pltpu.make_async_copy(src, dst, sems.at[i])
        for i, (src, dst) in enumerate(((wg, vg), (wu, vu), (wd, vd)))
    ]
    for copy in copies:
        copy.start()
    mine = pl.multiple_of(tp * half_rows, half_rows)
    other = pl.multiple_of((1 - tp) * half_rows, half_rows)
    rows[pl.ds(mine, half_rows), :] = a0[...]
    rows[pl.ds(other, half_rows), :] = a1[...]
    rows[pl.ds(2 * half_rows + mine, half_rows), :] = b0[...]
    rows[pl.ds(2 * half_rows + other, half_rows), :] = b1[...]
    tail = rows[:, model_width:].astype(jnp.float32)
    lane = lax.broadcasted_iota(jnp.int32, tail.shape, 1)
    scale = jnp.where(lane == expert, 256.0, jnp.where(lane == expert + expert_count, 1.0, 0.0))
    weight = jnp.sum(tail * scale, axis=1, keepdims=True) * (1.0 / 65536.0)
    x = rows[:, :model_width]
    copies[0].wait()
    gate_pre = jnp.dot(x, vg[...], preferred_element_type=jnp.float32)
    copies[1].wait()
    up_pre = jnp.dot(x, vu[...], preferred_element_type=jnp.float32)
    act = ((up_pre + 1.0) * gate_pre * jax.nn.sigmoid(1.702 * gate_pre)).astype(jnp.bfloat16)
    copies[2].wait()
    contract = (((1,), (1,)), ((), ()))
    theirs = vd[pl.ds(pl.multiple_of((1 - tp) * half_width, 16), half_width), :]
    out = lax.dot_general(act, theirs, contract, preferred_element_type=jnp.float32) * weight
    send[...] = out.astype(jnp.bfloat16)
    ours = vd[pl.ds(pl.multiple_of(tp * half_width, 16), half_width), :]
    out = lax.dot_general(act, ours, contract, preferred_element_type=jnp.float32) * weight
    keep_a[...] = out[: 2 * half_rows]
    keep_b[...] = out[2 * half_rows :]


def experts(expert_count, place, a0, a1, b0, b1, wg, wu, wd):
    half_rows, width = a0.shape
    model_width, slice_width = wg.shape
    half_width = model_width // 2
    block = 2 * half_rows
    vmem = pl.BlockSpec(memory_space=pltpu.VMEM)
    hbm = pl.BlockSpec(memory_space=pl.ANY)
    return pl.pallas_call(
        functools.partial(expert_kernel, expert_count),
        out_shape=(
            jax.ShapeDtypeStruct((block, half_width), jnp.float32),
            jax.ShapeDtypeStruct((block, half_width), jnp.float32),
            jax.ShapeDtypeStruct((2 * block, half_width), jnp.bfloat16),
        ),
        in_specs=[pl.BlockSpec(memory_space=pltpu.SMEM)] + [vmem] * 4 + [hbm] * 3,
        out_specs=(vmem, vmem, vmem),
        scratch_shapes=[
            pltpu.VMEM((model_width, slice_width), jnp.bfloat16),
            pltpu.VMEM((model_width, slice_width), jnp.bfloat16),
            pltpu.VMEM((model_width, slice_width), jnp.bfloat16),
            pltpu.VMEM((2 * block, width), jnp.bfloat16),
            pltpu.SemaphoreType.DMA((3,)),
        ],
        compiler_params=pltpu.CompilerParams(vmem_limit_bytes=32 * 1024 * 1024),
        cost_estimate=pl.CostEstimate(
            flops=2 * 2 * block * model_width * slice_width * 3,
            bytes_accessed=3 * model_width * slice_width * 2 + 4 * block * width * 2,
            transcendentals=2 * block * slice_width,
        ),
    )(place, a0, a1, b0, b1, wg, wu, wd)


def gathered(hidden, expert_ids, gate_units, w_gate, w_up, w_down):
    token_count, model_width = hidden.shape
    half_rows = token_count // 2
    tp = lax.axis_index("tp")
    expert_count = lax.axis_size("seq") * lax.axis_size("tp")
    expert = lax.axis_index("seq") * lax.axis_size("tp") + tp
    place = jnp.stack([tp, expert]).astype(jnp.int32)
    named = expert_ids[:, :, None] == jnp.arange(expert_count, dtype=jnp.int32)[None, None, :]
    units = jnp.sum(jnp.where(named, gate_units[:, :, None], 0), axis=1)
    payload = jnp.concatenate(
        [hidden, (units // 256).astype(jnp.bfloat16), (units % 256).astype(jnp.bfloat16)], axis=1
    )
    own = lax.dynamic_slice_in_dim(payload, tp * half_rows, half_rows, 0)
    own_rest = lax.dynamic_slice_in_dim(payload, (1 - tp) * half_rows, half_rows, 0)

    def z(x, k):
        return lax.ppermute(x, "seq", [(i, i ^ k) for i in range(lax.axis_size("seq"))])

    def swap(x, axis):
        return lax.ppermute(x, axis, [(0, 1), (1, 0)])

    near = {0: own}
    near[3] = z(own, 3)
    near[1] = z(own, 1)
    near[2] = z(near[3], 1)
    far = {k: swap(near[k], "ep") for k in (0, 1, 3, 2)}
    rest = {k: swap(near[k], "tp") for k in (1, 3, 2)}
    rest[0] = own_rest
    far_rest = {k: swap(far[k], "tp") for k in (0, 1, 3, 2)}
    total = None
    for k in (0, 1, 3, 2):
        keep_a, keep_b, send = experts(
            expert_count, place, near[k], rest[k], far[k], far_rest[k], w_gate[0], w_up[0], w_down[0]
        )
        came = swap(send, "tp").astype(jnp.float32)
        cross = swap((keep_b + came[token_count:]).astype(jnp.bfloat16), "ep")
        here = keep_a + came[:token_count] + cross.astype(jnp.float32)
        if k:
            here = z(here.astype(jnp.bfloat16), k).astype(jnp.float32)
        total = here if total is None else total + here
    return total.astype(jnp.bfloat16)


def solution(mesh):
    def local(*args):
        token_count = args[0].shape[0]
        seq, ep, tp = (mesh.shape[name] for name in ("seq", "ep", "tp"))
        dense = capacity_of(token_count, seq * tp) * tp >= token_count
        if dense and (seq, ep, tp) == (4, 2, 2):
            return gathered(*args)
        return routed(*args)

    return jax.shard_map(
        local,
        mesh=mesh,
        in_specs=(
            P(("groups", "seq", "ep"), None),
            P(("groups", "seq", "ep"), None),
            P(("groups", "seq", "ep"), None),
            P(("seq", "tp"), None, "ep"),
            P(("seq", "tp"), None, "ep"),
            P(("seq", "tp"), None, "ep"),
        ),
        out_specs=P(("groups", "seq", "ep"), "tp"),
        check_vma=False,
    )
```

```python
import functools

import jax
import jax.numpy as jnp
from jax import lax
from jax.experimental import pallas as pl
from jax.experimental.pallas import tpu as pltpu
from jax.sharding import PartitionSpec as P

TOP = 4


def slice_output(rows_in, gate_cols, up_cols, down_cols):
    gate_pre = jnp.dot(rows_in, gate_cols, preferred_element_type=jnp.float32)
    up_pre = jnp.dot(rows_in, up_cols, preferred_element_type=jnp.float32)
    activation = ((up_pre + 1.0) * gate_pre * jax.nn.sigmoid(1.702 * gate_pre)).astype(jnp.bfloat16)
    return lax.dot_general(
        activation, down_cols, (((1,), (1,)), ((), ())), preferred_element_type=jnp.float32
    ).astype(jnp.bfloat16)


def capacity_of(token_count, expert_count):
    return max(2, (token_count * TOP * 11 + expert_count * 8 - 1) // (expert_count * 8))


def routed(hidden, expert_ids, gate_units, w_gate, w_up, w_down):
    token_count, model_width = hidden.shape
    seq_count = lax.axis_size("seq")
    ep_count = lax.axis_size("ep")
    tp_count = lax.axis_size("tp")
    half_width = model_width // tp_count
    my_half = lax.axis_index("tp")
    expert_count = seq_count * tp_count
    capacity = capacity_of(token_count, expert_count)
    flat_ids = expert_ids.reshape(-1)
    onehot_ids = (flat_ids[:, None] == jnp.arange(expert_count, dtype=jnp.int32)[None, :]).astype(
        jnp.int32
    )
    slot_rank = jnp.sum((jnp.cumsum(onehot_ids, axis=0) - 1) * onehot_ids, axis=1)
    owner_seq = flat_ids // tp_count
    owner_half = flat_ids % tp_count
    send_row = jnp.where(owner_half == my_half, owner_seq * capacity + slot_rank, -1)
    selector = jnp.arange(seq_count * capacity, dtype=jnp.int32)[:, None] == send_row[None, :]
    selector = jnp.any(selector.reshape(seq_count * capacity, token_count, TOP), axis=2).astype(
        jnp.bfloat16
    )
    outgoing = jnp.dot(selector, hidden, preferred_element_type=jnp.float32).astype(jnp.bfloat16)
    outgoing = outgoing.reshape(seq_count, capacity, model_width)
    column_of = (owner_half * seq_count + owner_seq) * capacity + slot_rank
    gate_share = gate_units.reshape(-1).astype(jnp.float32) / 65536.0
    column_ids = jnp.arange(tp_count * seq_count * capacity, dtype=jnp.int32)
    combiner = jnp.where(column_ids[None, :] == column_of[:, None], gate_share[:, None], 0.0)
    combiner = jnp.sum(combiner.reshape(token_count, TOP, -1), axis=1)
    copied = jnp.broadcast_to(outgoing[:, None], (seq_count, ep_count, capacity, model_width))
    copied = copied.reshape(seq_count * ep_count, capacity, model_width)
    arrived = lax.all_to_all(copied, ("seq", "ep"), split_axis=0, concat_axis=0, tiled=True)
    slice_rows = slice_output(arrived.reshape(-1, model_width), w_gate[0], w_up[0], w_down[0])
    slice_rows = slice_rows.reshape(seq_count * ep_count, capacity, model_width)
    came_back = lax.all_to_all(
        lax.all_to_all(slice_rows, ("seq", "ep"), split_axis=0, concat_axis=0, tiled=True),
        "tp",
        split_axis=2,
        concat_axis=0,
        tiled=True,
    )
    came_back = came_back.reshape(tp_count, seq_count, ep_count, capacity, half_width)
    returned = jnp.sum(came_back.astype(jnp.float32), axis=2).astype(jnp.bfloat16)
    result_rows = returned.reshape(-1, half_width).astype(jnp.float32)
    moe_out = jnp.dot(
        combiner, result_rows, precision=lax.Precision.HIGHEST, preferred_element_type=jnp.float32
    )
    return moe_out.astype(jnp.bfloat16)


def expert_kernel(expert_count, count, place_ref, *refs):
    ins, weights = refs[:count], refs[count : count + 2]
    outs, rows = refs[count + 2 : -1], refs[-1]
    model_width = outs[0].shape[1]
    first = 0
    for ref in ins:
        rows[first : first + ref.shape[0], :] = ref[...]
        first += ref.shape[0]
    tail = rows[:, model_width:].astype(jnp.float32)
    lane = lax.broadcasted_iota(jnp.int32, tail.shape, 1)
    x = rows[:, :model_width]
    total = None
    for i in range(2):
        wg, wu, wd = (weights[i].at[j] for j in range(3))
        expert = place_ref[i]
        scale = jnp.where(lane == expert, 256.0, jnp.where(lane == expert + expert_count, 1.0, 0.0))
        weight = jnp.sum(tail * scale, axis=1, keepdims=True) * (1.0 / 65536.0)
        gate_pre = jnp.dot(x, wg[...], preferred_element_type=jnp.float32)
        up_pre = jnp.dot(x, wu[...], preferred_element_type=jnp.float32)
        act = ((up_pre + 1.0) * gate_pre * jax.nn.sigmoid(1.702 * gate_pre)).astype(jnp.bfloat16)
        out = lax.dot_general(
            act, wd[...], (((1,), (1,)), ((), ())), preferred_element_type=jnp.float32
        )
        total = out * weight if total is None else total + out * weight
    half_rows = outs[0].shape[0]
    for i, ref in enumerate(outs):
        ref[...] = total[i * half_rows : (i + 1) * half_rows].astype(ref.dtype)


def experts(expert_count, place, model_width, blocks, weights):
    half_rows, width = blocks[0].shape
    slice_width = weights[0].shape[2]
    vmem = pl.BlockSpec(memory_space=pltpu.VMEM)
    count = len(blocks)
    rows = count * half_rows
    return pl.pallas_call(
        functools.partial(expert_kernel, expert_count, count),
        out_shape=tuple(
            jax.ShapeDtypeStruct((half_rows, model_width), (jnp.float32, jnp.bfloat16)[i % 2])
            for i in range(count)
        ),
        in_specs=[pl.BlockSpec(memory_space=pltpu.SMEM)] + [vmem] * (count + 2),
        out_specs=tuple([vmem] * count),
        scratch_shapes=[pltpu.VMEM((rows, width), jnp.bfloat16)],
        compiler_params=pltpu.CompilerParams(vmem_limit_bytes=20 * 1024 * 1024),
        cost_estimate=pl.CostEstimate(
            flops=2 * rows * model_width * slice_width * 6,
            bytes_accessed=4 * rows * width,
            transcendentals=2 * rows * slice_width,
        ),
    )(place, *blocks, *weights)


def prepare_kernel(place_ref, *refs):
    own, held, hidden, ids, units, rows, sems = refs[6:]
    targets = (hidden, ids, units, *(held.at[i] for i in range(3)))
    copies = [pltpu.make_async_copy(refs[i], to, sems.at[i]) for i, to in enumerate(targets)]
    for copy in copies:
        copy.start()
    model_width, token_count = hidden.shape
    expert_count = (own.shape[1] - model_width) // 2
    half_rows = own.shape[0]
    expert = lax.broadcasted_iota(jnp.int32, (expert_count, token_count), 0)
    shares = jnp.zeros((expert_count, token_count), jnp.int32)
    copies[1].wait()
    copies[2].wait()
    for c in range(ids.shape[0]):
        shares += jnp.where(ids[c : c + 1, :] == expert, units[c : c + 1, :], 0)
    digits = jnp.concatenate([shares // 256, shares % 256], axis=0).astype(jnp.float32)
    rows[:, model_width:] = digits.T.astype(jnp.bfloat16)
    copies[0].wait()
    rows[:, :model_width] = hidden[...].T
    own[...] = rows[pl.ds(pl.multiple_of(place_ref[2] * half_rows, half_rows), half_rows), :]
    for copy in copies[3:]:
        copy.wait()


def prepare(place, expert_count, hidden, expert_ids, gate_units, weights):
    token_count, model_width = hidden.shape
    width = model_width + 2 * expert_count
    vmem = pl.BlockSpec(memory_space=pltpu.VMEM)
    return pl.pallas_call(
        prepare_kernel,
        out_shape=(
            jax.ShapeDtypeStruct((token_count // 2, width), hidden.dtype),
            jax.ShapeDtypeStruct((len(weights), *weights[0].shape), weights[0].dtype),
        ),
        in_specs=[pl.BlockSpec(memory_space=pltpu.SMEM)] + [pl.BlockSpec(memory_space=pl.ANY)] * 6,
        out_specs=(vmem, vmem),
        scratch_shapes=[
            pltpu.VMEM((model_width, token_count), hidden.dtype),
            pltpu.VMEM(expert_ids.T.shape, jnp.int32),
            pltpu.VMEM(gate_units.T.shape, jnp.int32),
            pltpu.VMEM((token_count, width), hidden.dtype),
            pltpu.SemaphoreType.DMA((6,)),
        ],
        compiler_params=pltpu.CompilerParams(vmem_limit_bytes=16 * 1024 * 1024),
    )(
        place,
        *[
            pltpu.with_memory_space_constraint(x, pltpu.HBM)
            for x in (hidden.T, expert_ids.T, gate_units.T, *weights)
        ],
    )


def hold_kernel(*refs):
    del refs


def hold(*arrays):
    return pl.pallas_call(
        hold_kernel,
        out_shape=tuple(jax.ShapeDtypeStruct(x.shape, x.dtype) for x in arrays),
        in_specs=[pl.BlockSpec(memory_space=pl.ANY)] * len(arrays),
        out_specs=tuple([pl.BlockSpec(memory_space=pl.ANY)] * len(arrays)),
        input_output_aliases={i: i for i in range(len(arrays))},
        compiler_params=pltpu.CompilerParams(vmem_limit_bytes=1024 * 1024),
    )(*arrays)


def gathered(hidden, expert_ids, gate_units, w_gate, w_up, w_down):
    token_count, model_width = hidden.shape
    half_rows = token_count // 2
    half_width = model_width // 2
    tp = lax.axis_index("tp")
    expert_count = lax.axis_size("seq") * lax.axis_size("tp")
    expert = lax.axis_index("seq") * lax.axis_size("tp") + tp
    place = jnp.stack([expert, expert + 1 - 2 * tp, tp]).astype(jnp.int32)

    def z(x, k):
        return lax.ppermute(x, "seq", [(i, i ^ k) for i in range(lax.axis_size("seq"))])

    def diagonal(x):
        flat = [(i, i ^ 3) for i in range(lax.axis_size("seq") * lax.axis_size("ep"))]
        return lax.ppermute(x, ("seq", "ep"), flat)

    def swap(x, axis):
        return lax.ppermute(x, axis, [(0, 1), (1, 0)])

    own, mine = prepare(
        place, expert_count, hidden, expert_ids, gate_units, (w_gate[0], w_up[0], w_down[0])
    )
    run = functools.partial(experts, expert_count, place, model_width)
    weights = (mine, swap(mine, "tp"))
    near3, near1, far0 = hold(z(own, 3), z(own, 1), swap(own, "ep"))
    far3, near2, far2 = swap(near3, "ep"), z(near3, 1), diagonal(near3)
    near1, far3, near2, far2, near3 = hold(near1, far3, near2, far2, near3)
    far1 = swap(near1, "ep")
    near_sum3, far_sum3, near_sum2, far_sum2 = run([near3, far3, near2, far2], weights)
    near_sum0, far_sum0, near_sum1, far_sum1 = run([own, far0, near1, far1], weights)

    def f32(x):
        return x.astype(jnp.float32)

    def bf16(x):
        return x.astype(jnp.bfloat16)

    merged = near_sum3 + f32(swap(far_sum3, "ep")) + f32(z(bf16(near_sum2), 1)) + f32(diagonal(far_sum2))
    total = (
        near_sum0
        + f32(swap(far_sum0, "ep"))
        + f32(z(bf16(near_sum1 + f32(swap(far_sum1, "ep"))), 1))
        + f32(z(bf16(merged), 3))
    )
    out = total.astype(jnp.bfloat16)
    give = lax.dynamic_slice_in_dim(out, (1 - tp) * half_width, half_width, 1)
    keep = lax.dynamic_slice_in_dim(out, tp * half_width, half_width, 1)
    get = swap(give, "tp")
    return jnp.where(tp == 0, jnp.concatenate([keep, get]), jnp.concatenate([get, keep]))


def solution(mesh):
    def local(*args):
        token_count = args[0].shape[0]
        seq, ep, tp = (mesh.shape[name] for name in ("seq", "ep", "tp"))
        dense = capacity_of(token_count, seq * tp) * tp >= token_count
        if dense and (seq, ep, tp) == (4, 2, 2):
            return gathered(*args)
        return routed(*args)

    return jax.shard_map(
        local,
        mesh=mesh,
        in_specs=(
            P(("groups", "seq", "ep"), None),
            P(("groups", "seq", "ep"), None),
            P(("groups", "seq", "ep"), None),
            P(("seq", "tp"), None, "ep"),
            P(("seq", "tp"), None, "ep"),
            P(("seq", "tp"), None, "ep"),
        ),
        out_specs=P(("groups", "seq", "ep"), "tp"),
        check_vma=False,
    )
```

```python
import functools

import jax
import jax.numpy as jnp
from jax import lax
from jax.experimental import pallas as pl
from jax.experimental.pallas import tpu as pltpu
from jax.sharding import PartitionSpec as P

TOP = 4


def slice_output(rows_in, gate_cols, up_cols, down_cols):
    gate_pre = jnp.dot(rows_in, gate_cols, preferred_element_type=jnp.float32)
    up_pre = jnp.dot(rows_in, up_cols, preferred_element_type=jnp.float32)
    activation = ((up_pre + 1.0) * gate_pre * jax.nn.sigmoid(1.702 * gate_pre)).astype(jnp.bfloat16)
    return lax.dot_general(
        activation, down_cols, (((1,), (1,)), ((), ())), preferred_element_type=jnp.float32
    ).astype(jnp.bfloat16)


def capacity_of(token_count, expert_count):
    return max(2, (token_count * TOP * 11 + expert_count * 8 - 1) // (expert_count * 8))


def routed(hidden, expert_ids, gate_units, w_gate, w_up, w_down):
    token_count, model_width = hidden.shape
    seq_count = lax.axis_size("seq")
    ep_count = lax.axis_size("ep")
    tp_count = lax.axis_size("tp")
    half_width = model_width // tp_count
    my_half = lax.axis_index("tp")
    expert_count = seq_count * tp_count
    capacity = capacity_of(token_count, expert_count)
    flat_ids = expert_ids.reshape(-1)
    onehot_ids = (flat_ids[:, None] == jnp.arange(expert_count, dtype=jnp.int32)[None, :]).astype(
        jnp.int32
    )
    slot_rank = jnp.sum((jnp.cumsum(onehot_ids, axis=0) - 1) * onehot_ids, axis=1)
    owner_seq = flat_ids // tp_count
    owner_half = flat_ids % tp_count
    send_row = jnp.where(owner_half == my_half, owner_seq * capacity + slot_rank, -1)
    selector = jnp.arange(seq_count * capacity, dtype=jnp.int32)[:, None] == send_row[None, :]
    selector = jnp.any(selector.reshape(seq_count * capacity, token_count, TOP), axis=2).astype(
        jnp.bfloat16
    )
    outgoing = jnp.dot(selector, hidden, preferred_element_type=jnp.float32).astype(jnp.bfloat16)
    outgoing = outgoing.reshape(seq_count, capacity, model_width)
    column_of = (owner_half * seq_count + owner_seq) * capacity + slot_rank
    gate_share = gate_units.reshape(-1).astype(jnp.float32) / 65536.0
    column_ids = jnp.arange(tp_count * seq_count * capacity, dtype=jnp.int32)
    combiner = jnp.where(column_ids[None, :] == column_of[:, None], gate_share[:, None], 0.0)
    combiner = jnp.sum(combiner.reshape(token_count, TOP, -1), axis=1)
    copied = jnp.broadcast_to(outgoing[:, None], (seq_count, ep_count, capacity, model_width))
    copied = copied.reshape(seq_count * ep_count, capacity, model_width)
    arrived = lax.all_to_all(copied, ("seq", "ep"), split_axis=0, concat_axis=0, tiled=True)
    slice_rows = slice_output(arrived.reshape(-1, model_width), w_gate[0], w_up[0], w_down[0])
    slice_rows = slice_rows.reshape(seq_count * ep_count, capacity, model_width)
    came_back = lax.all_to_all(
        lax.all_to_all(slice_rows, ("seq", "ep"), split_axis=0, concat_axis=0, tiled=True),
        "tp",
        split_axis=2,
        concat_axis=0,
        tiled=True,
    )
    came_back = came_back.reshape(tp_count, seq_count, ep_count, capacity, half_width)
    returned = jnp.sum(came_back.astype(jnp.float32), axis=2).astype(jnp.bfloat16)
    result_rows = returned.reshape(-1, half_width).astype(jnp.float32)
    moe_out = jnp.dot(
        combiner, result_rows, precision=lax.Precision.HIGHEST, preferred_element_type=jnp.float32
    )
    return moe_out.astype(jnp.bfloat16)


def expert_kernel(expert_count, count, place_ref, *refs):
    ins, weights = refs[:count], refs[count : count + 6]
    outs, rows = refs[count + 6 : -1], refs[-1]
    model_width = outs[0].shape[1]
    first = 0
    for ref in ins:
        rows[first : first + ref.shape[0], :] = ref[...]
        first += ref.shape[0]
    tail = rows[:, model_width:].astype(jnp.float32)
    lane = lax.broadcasted_iota(jnp.int32, tail.shape, 1)
    x = rows[:, :model_width]
    total = None
    for i in range(2):
        wg, wu, wd = weights[3 * i : 3 * i + 3]
        expert = place_ref[i]
        scale = jnp.where(lane == expert, 256.0, jnp.where(lane == expert + expert_count, 1.0, 0.0))
        weight = jnp.sum(tail * scale, axis=1, keepdims=True) * (1.0 / 65536.0)
        gate_pre = jnp.dot(x, wg[...], preferred_element_type=jnp.float32)
        up_pre = jnp.dot(x, wu[...], preferred_element_type=jnp.float32)
        act = ((up_pre + 1.0) * gate_pre * jax.nn.sigmoid(1.702 * gate_pre)).astype(jnp.bfloat16)
        out = lax.dot_general(
            act, wd[...], (((1,), (1,)), ((), ())), preferred_element_type=jnp.float32
        )
        total = out * weight if total is None else total + out * weight
    half_rows = outs[0].shape[0]
    for i, ref in enumerate(outs):
        ref[...] = total[i * half_rows : (i + 1) * half_rows].astype(ref.dtype)


def experts(expert_count, place, model_width, blocks, weights):
    half_rows, width = blocks[0].shape
    slice_width = weights[0].shape[1]
    vmem = pl.BlockSpec(memory_space=pltpu.VMEM)
    count = len(blocks)
    rows = count * half_rows
    return pl.pallas_call(
        functools.partial(expert_kernel, expert_count, count),
        out_shape=tuple(
            jax.ShapeDtypeStruct((half_rows, model_width), (jnp.float32, jnp.bfloat16)[i % 2])
            for i in range(count)
        ),
        in_specs=[pl.BlockSpec(memory_space=pltpu.SMEM)] + [vmem] * (count + 6),
        out_specs=tuple([vmem] * count),
        scratch_shapes=[pltpu.VMEM((rows, width), jnp.bfloat16)],
        compiler_params=pltpu.CompilerParams(vmem_limit_bytes=20 * 1024 * 1024),
        cost_estimate=pl.CostEstimate(
            flops=2 * rows * model_width * slice_width * 6,
            bytes_accessed=4 * rows * width,
            transcendentals=2 * rows * slice_width,
        ),
    )(place, *blocks, *weights)


def prepare_kernel(place_ref, *refs):
    own, hidden, ids, units, rows, sems = refs[3:]
    copies = [pltpu.make_async_copy(refs[i], refs[i + 4], sems.at[i]) for i in range(3)]
    for copy in copies:
        copy.start()
    model_width, token_count = hidden.shape
    expert_count = (own.shape[1] - model_width) // 2
    half_rows = own.shape[0]
    expert = lax.broadcasted_iota(jnp.int32, (expert_count, token_count), 0)
    shares = jnp.zeros((expert_count, token_count), jnp.int32)
    copies[1].wait()
    copies[2].wait()
    for c in range(ids.shape[0]):
        shares += jnp.where(ids[c : c + 1, :] == expert, units[c : c + 1, :], 0)
    digits = jnp.concatenate([shares // 256, shares % 256], axis=0).astype(jnp.float32)
    rows[:, model_width:] = digits.T.astype(jnp.bfloat16)
    copies[0].wait()
    rows[:, :model_width] = hidden[...].T
    own[...] = rows[pl.ds(pl.multiple_of(place_ref[2] * half_rows, half_rows), half_rows), :]


def prepare(place, expert_count, hidden, expert_ids, gate_units):
    token_count, model_width = hidden.shape
    width = model_width + 2 * expert_count
    arrays = hidden.T, expert_ids.T, gate_units.T
    return pl.pallas_call(
        prepare_kernel,
        out_shape=jax.ShapeDtypeStruct((token_count // 2, width), hidden.dtype),
        in_specs=[pl.BlockSpec(memory_space=pltpu.SMEM)] + [pl.BlockSpec(memory_space=pl.ANY)] * 3,
        out_specs=pl.BlockSpec(memory_space=pltpu.VMEM),
        scratch_shapes=[pltpu.VMEM(x.shape, x.dtype) for x in arrays]
        + [pltpu.VMEM((token_count, width), hidden.dtype), pltpu.SemaphoreType.DMA((3,))],
        compiler_params=pltpu.CompilerParams(vmem_limit_bytes=8 * 1024 * 1024),
    )(place, *[pltpu.with_memory_space_constraint(x, pltpu.HBM) for x in arrays])


def stage_kernel(count, *refs):
    ins, outs, sems = refs[:count], refs[-count - 1 : -1], refs[-1]
    copies = [pltpu.make_async_copy(ins[i], outs[i], sems.at[i]) for i in range(count)]
    for copy in copies:
        copy.start()
    for copy in copies:
        copy.wait()


def stage(after, *arrays):
    return pl.pallas_call(
        functools.partial(stage_kernel, len(arrays)),
        out_shape=tuple(jax.ShapeDtypeStruct(x.shape, x.dtype) for x in arrays),
        in_specs=[pl.BlockSpec(memory_space=pl.ANY)] * (len(arrays) + 1),
        out_specs=tuple([pl.BlockSpec(memory_space=pltpu.VMEM)] * len(arrays)),
        scratch_shapes=[pltpu.SemaphoreType.DMA((len(arrays),))],
        compiler_params=pltpu.CompilerParams(vmem_limit_bytes=8 * 1024 * 1024),
        cost_estimate=pl.CostEstimate(
            flops=0, bytes_accessed=2 * sum(x.size for x in arrays), transcendentals=0
        ),
    )(*[pltpu.with_memory_space_constraint(x, pltpu.HBM) for x in arrays], after)


def hold_kernel(*refs):
    del refs


def hold(*arrays):
    return pl.pallas_call(
        hold_kernel,
        out_shape=tuple(jax.ShapeDtypeStruct(x.shape, x.dtype) for x in arrays),
        in_specs=[pl.BlockSpec(memory_space=pl.ANY)] * len(arrays),
        out_specs=tuple([pl.BlockSpec(memory_space=pl.ANY)] * len(arrays)),
        input_output_aliases={i: i for i in range(len(arrays))},
        compiler_params=pltpu.CompilerParams(vmem_limit_bytes=1024 * 1024),
    )(*arrays)


def gathered(hidden, expert_ids, gate_units, w_gate, w_up, w_down):
    token_count, model_width = hidden.shape
    half_rows = token_count // 2
    half_width = model_width // 2
    tp = lax.axis_index("tp")
    expert_count = lax.axis_size("seq") * lax.axis_size("tp")
    expert = lax.axis_index("seq") * lax.axis_size("tp") + tp
    place = jnp.stack([expert, expert + 1 - 2 * tp, tp]).astype(jnp.int32)

    def z(x, k):
        return lax.ppermute(x, "seq", [(i, i ^ k) for i in range(lax.axis_size("seq"))])

    def diagonal(x):
        flat = [(i, i ^ 3) for i in range(lax.axis_size("seq") * lax.axis_size("ep"))]
        return lax.ppermute(x, ("seq", "ep"), flat)

    def swap(x, axis):
        return lax.ppermute(x, axis, [(0, 1), (1, 0)])

    own = prepare(place, expert_count, hidden, expert_ids, gate_units)
    run = functools.partial(experts, expert_count, place, model_width)
    gate2, up2 = swap(w_gate[0], "tp"), swap(w_up[0], "tp")
    near3, near1, far0, down1, gate1, up1 = hold(
        z(own, 3),
        z(own, 1),
        swap(own, "ep"),
        *stage(own, w_down[0]),
        *stage(own, w_gate[0], w_up[0]),
    )
    held3, gate2, up2 = hold(near3, gate2, up2)
    far3, near2, far2 = swap(near3, "ep"), z(near3, 1), diagonal(held3)
    down2 = swap(down1, "tp")
    weights = gate1, up1, down1, gate2, up2, down2
    near_sum3, far_sum3 = run([near3, far3], weights)
    far_sum3, near1 = hold(far_sum3, near1)
    near2, far2, near_sum3 = hold(near2, far2, near_sum3)
    near_sum2, far_sum2 = run([near2, far2], weights)
    back3, far1, own = hold(swap(far_sum3, "ep"), swap(near1, "ep"), own)
    near_sum0, far_sum0, near_sum1, far_sum1 = run([own, far0, near1, far1], weights)

    def f32(x):
        return x.astype(jnp.float32)

    def bf16(x):
        return x.astype(jnp.bfloat16)

    merged = near_sum3 + f32(back3) + f32(z(bf16(near_sum2), 1)) + f32(diagonal(far_sum2))
    back1, far_sum0 = hold(swap(far_sum1, "ep"), far_sum0)
    total = (
        near_sum0
        + f32(swap(far_sum0, "ep"))
        + f32(z(bf16(near_sum1 + f32(back1)), 1))
        + f32(z(bf16(merged), 3))
    )
    out = total.astype(jnp.bfloat16)
    give = lax.dynamic_slice_in_dim(out, (1 - tp) * half_width, half_width, 1)
    keep = lax.dynamic_slice_in_dim(out, tp * half_width, half_width, 1)
    get = swap(give, "tp")
    return jnp.where(tp == 0, jnp.concatenate([keep, get]), jnp.concatenate([get, keep]))


def solution(mesh):
    def local(*args):
        token_count = args[0].shape[0]
        seq, ep, tp = (mesh.shape[name] for name in ("seq", "ep", "tp"))
        dense = capacity_of(token_count, seq * tp) * tp >= token_count
        if dense and (seq, ep, tp) == (4, 2, 2):
            return gathered(*args)
        return routed(*args)

    return jax.shard_map(
        local,
        mesh=mesh,
        in_specs=(
            P(("groups", "seq", "ep"), None),
            P(("groups", "seq", "ep"), None),
            P(("groups", "seq", "ep"), None),
            P(("seq", "tp"), None, "ep"),
            P(("seq", "tp"), None, "ep"),
            P(("seq", "tp"), None, "ep"),
        ),
        out_specs=P(("groups", "seq", "ep"), "tp"),
        check_vma=False,
    )
```

```python
import functools

import jax
import jax.numpy as jnp
from jax import lax
from jax.experimental import pallas as pl
from jax.experimental.pallas import tpu as pltpu
from jax.sharding import PartitionSpec as P

TOP = 4


def slice_output(rows_in, gate_cols, up_cols, down_cols):
    gate_pre = jnp.dot(rows_in, gate_cols, preferred_element_type=jnp.float32)
    up_pre = jnp.dot(rows_in, up_cols, preferred_element_type=jnp.float32)
    activation = ((up_pre + 1.0) * gate_pre * jax.nn.sigmoid(1.702 * gate_pre)).astype(jnp.bfloat16)
    return lax.dot_general(
        activation, down_cols, (((1,), (1,)), ((), ())), preferred_element_type=jnp.float32
    ).astype(jnp.bfloat16)


def capacity_of(token_count, expert_count):
    return max(2, (token_count * TOP * 11 + expert_count * 8 - 1) // (expert_count * 8))


def routed(hidden, expert_ids, gate_units, w_gate, w_up, w_down):
    token_count, model_width = hidden.shape
    seq_count = lax.axis_size("seq")
    ep_count = lax.axis_size("ep")
    tp_count = lax.axis_size("tp")
    half_width = model_width // tp_count
    my_half = lax.axis_index("tp")
    expert_count = seq_count * tp_count
    capacity = capacity_of(token_count, expert_count)
    flat_ids = expert_ids.reshape(-1)
    onehot_ids = (flat_ids[:, None] == jnp.arange(expert_count, dtype=jnp.int32)[None, :]).astype(
        jnp.int32
    )
    slot_rank = jnp.sum((jnp.cumsum(onehot_ids, axis=0) - 1) * onehot_ids, axis=1)
    owner_seq = flat_ids // tp_count
    owner_half = flat_ids % tp_count
    send_row = jnp.where(owner_half == my_half, owner_seq * capacity + slot_rank, -1)
    selector = jnp.arange(seq_count * capacity, dtype=jnp.int32)[:, None] == send_row[None, :]
    selector = jnp.any(selector.reshape(seq_count * capacity, token_count, TOP), axis=2).astype(
        jnp.bfloat16
    )
    outgoing = jnp.dot(selector, hidden, preferred_element_type=jnp.float32).astype(jnp.bfloat16)
    outgoing = outgoing.reshape(seq_count, capacity, model_width)
    column_of = (owner_half * seq_count + owner_seq) * capacity + slot_rank
    gate_share = gate_units.reshape(-1).astype(jnp.float32) / 65536.0
    column_ids = jnp.arange(tp_count * seq_count * capacity, dtype=jnp.int32)
    combiner = jnp.where(column_ids[None, :] == column_of[:, None], gate_share[:, None], 0.0)
    combiner = jnp.sum(combiner.reshape(token_count, TOP, -1), axis=1)
    copied = jnp.broadcast_to(outgoing[:, None], (seq_count, ep_count, capacity, model_width))
    copied = copied.reshape(seq_count * ep_count, capacity, model_width)
    arrived = lax.all_to_all(copied, ("seq", "ep"), split_axis=0, concat_axis=0, tiled=True)
    slice_rows = slice_output(arrived.reshape(-1, model_width), w_gate[0], w_up[0], w_down[0])
    slice_rows = slice_rows.reshape(seq_count * ep_count, capacity, model_width)
    came_back = lax.all_to_all(
        lax.all_to_all(slice_rows, ("seq", "ep"), split_axis=0, concat_axis=0, tiled=True),
        "tp",
        split_axis=2,
        concat_axis=0,
        tiled=True,
    )
    came_back = came_back.reshape(tp_count, seq_count, ep_count, capacity, half_width)
    returned = jnp.sum(came_back.astype(jnp.float32), axis=2).astype(jnp.bfloat16)
    result_rows = returned.reshape(-1, half_width).astype(jnp.float32)
    moe_out = jnp.dot(
        combiner, result_rows, precision=lax.Precision.HIGHEST, preferred_element_type=jnp.float32
    )
    return moe_out.astype(jnp.bfloat16)


def expert_kernel(expert_count, count, place_ref, *refs):
    ins, weights = refs[:count], refs[count : count + 6]
    outs, rows = refs[count + 6 : -1], refs[-1]
    model_width = outs[0].shape[1]
    first = 0
    for ref in ins:
        rows[first : first + ref.shape[0], :] = ref[...]
        first += ref.shape[0]
    tail = rows[:, model_width:].astype(jnp.float32)
    lane = lax.broadcasted_iota(jnp.int32, tail.shape, 1)
    x = rows[:, :model_width]
    total = None
    for i in range(2):
        wg, wu, wd = weights[3 * i : 3 * i + 3]
        expert = place_ref[i]
        scale = jnp.where(lane == expert, 256.0, jnp.where(lane == expert + expert_count, 1.0, 0.0))
        weight = jnp.sum(tail * scale, axis=1, keepdims=True) * (1.0 / 65536.0)
        gate_pre = jnp.dot(x, wg[...], preferred_element_type=jnp.float32)
        up_pre = jnp.dot(x, wu[...], preferred_element_type=jnp.float32)
        act = ((up_pre + 1.0) * gate_pre * jax.nn.sigmoid(1.702 * gate_pre)).astype(jnp.bfloat16)
        out = lax.dot_general(
            act, wd[...], (((1,), (1,)), ((), ())), preferred_element_type=jnp.float32
        )
        total = out * weight if total is None else total + out * weight
    half_rows = outs[0].shape[0]
    for i, ref in enumerate(outs):
        ref[...] = total[i * half_rows : (i + 1) * half_rows].astype(ref.dtype)


def experts(expert_count, place, model_width, blocks, weights):
    half_rows, width = blocks[0].shape
    slice_width = weights[0].shape[1]
    vmem = pl.BlockSpec(memory_space=pltpu.VMEM)
    count = len(blocks)
    rows = count * half_rows
    return pl.pallas_call(
        functools.partial(expert_kernel, expert_count, count),
        out_shape=tuple(
            jax.ShapeDtypeStruct((half_rows, model_width), (jnp.float32, jnp.bfloat16)[i % 2])
            for i in range(count)
        ),
        in_specs=[pl.BlockSpec(memory_space=pltpu.SMEM)] + [vmem] * (count + 6),
        out_specs=tuple([vmem] * count),
        scratch_shapes=[pltpu.VMEM((rows, width), jnp.bfloat16)],
        compiler_params=pltpu.CompilerParams(vmem_limit_bytes=20 * 1024 * 1024),
        cost_estimate=pl.CostEstimate(
            flops=2 * rows * model_width * slice_width * 6,
            bytes_accessed=4 * rows * width,
            transcendentals=2 * rows * slice_width,
        ),
    )(place, *blocks, *weights)


def prepare_kernel(place_ref, *refs):
    own, hidden, ids, units, rows, sems = refs[3:]
    copies = [pltpu.make_async_copy(refs[i], refs[i + 4], sems.at[i]) for i in range(3)]
    for copy in copies:
        copy.start()
    model_width, token_count = hidden.shape
    expert_count = (own.shape[1] - model_width) // 2
    half_rows = own.shape[0]
    expert = lax.broadcasted_iota(jnp.int32, (expert_count, token_count), 0)
    shares = jnp.zeros((expert_count, token_count), jnp.int32)
    copies[1].wait()
    copies[2].wait()
    for c in range(ids.shape[0]):
        shares += jnp.where(ids[c : c + 1, :] == expert, units[c : c + 1, :], 0)
    digits = jnp.concatenate([shares // 256, shares % 256], axis=0).astype(jnp.float32)
    rows[:, model_width:] = digits.T.astype(jnp.bfloat16)
    copies[0].wait()
    rows[:, :model_width] = hidden[...].T
    own[...] = rows[pl.ds(pl.multiple_of(place_ref[2] * half_rows, half_rows), half_rows), :]


def prepare(place, expert_count, hidden, expert_ids, gate_units):
    token_count, model_width = hidden.shape
    width = model_width + 2 * expert_count
    arrays = hidden.T, expert_ids.T, gate_units.T
    return pl.pallas_call(
        prepare_kernel,
        out_shape=jax.ShapeDtypeStruct((token_count // 2, width), hidden.dtype),
        in_specs=[pl.BlockSpec(memory_space=pltpu.SMEM)] + [pl.BlockSpec(memory_space=pl.ANY)] * 3,
        out_specs=pl.BlockSpec(memory_space=pltpu.VMEM),
        scratch_shapes=[pltpu.VMEM(x.shape, x.dtype) for x in arrays]
        + [pltpu.VMEM((token_count, width), hidden.dtype), pltpu.SemaphoreType.DMA((3,))],
        compiler_params=pltpu.CompilerParams(vmem_limit_bytes=8 * 1024 * 1024),
    )(place, *[pltpu.with_memory_space_constraint(x, pltpu.HBM) for x in arrays])


def stage_kernel(count, *refs):
    ins, outs, sems = refs[:count], refs[-count - 1 : -1], refs[-1]
    copies = [pltpu.make_async_copy(ins[i], outs[i], sems.at[i]) for i in range(count)]
    for copy in copies:
        copy.start()
    for copy in copies:
        copy.wait()


def stage(after, *arrays):
    return pl.pallas_call(
        functools.partial(stage_kernel, len(arrays)),
        out_shape=tuple(jax.ShapeDtypeStruct(x.shape, x.dtype) for x in arrays),
        in_specs=[pl.BlockSpec(memory_space=pl.ANY)] * (len(arrays) + 1),
        out_specs=tuple([pl.BlockSpec(memory_space=pltpu.VMEM)] * len(arrays)),
        scratch_shapes=[pltpu.SemaphoreType.DMA((len(arrays),))],
        compiler_params=pltpu.CompilerParams(vmem_limit_bytes=8 * 1024 * 1024),
        cost_estimate=pl.CostEstimate(
            flops=0, bytes_accessed=2 * sum(x.size for x in arrays), transcendentals=0
        ),
    )(*[pltpu.with_memory_space_constraint(x, pltpu.HBM) for x in arrays], after)


def halves_kernel(place_ref, *refs):
    ins, (here, there) = refs[:-2], refs[-2:]
    half_width = here.shape[1]
    total = ins[0][...]
    for ref in ins[1:]:
        total = total + ref[...].astype(jnp.float32)
    first = place_ref[2] == 0
    left, right = total[:, :half_width], total[:, half_width:]
    here[...] = jnp.where(first, left, right).astype(here.dtype)
    there[...] = jnp.where(first, right, left).astype(there.dtype)


def halves(place, kept, *arrays):
    rows, width = arrays[0].shape
    vmem = pl.BlockSpec(memory_space=pltpu.VMEM)
    return pl.pallas_call(
        halves_kernel,
        out_shape=tuple(
            jax.ShapeDtypeStruct((rows, width // 2), dtype) for dtype in (kept, jnp.bfloat16)
        ),
        in_specs=[pl.BlockSpec(memory_space=pltpu.SMEM)] + [vmem] * len(arrays),
        out_specs=(vmem, vmem),
        compiler_params=pltpu.CompilerParams(vmem_limit_bytes=8 * 1024 * 1024),
    )(place, *arrays)


def hold_kernel(*refs):
    del refs


def hold(*arrays):
    return pl.pallas_call(
        hold_kernel,
        out_shape=tuple(jax.ShapeDtypeStruct(x.shape, x.dtype) for x in arrays),
        in_specs=[pl.BlockSpec(memory_space=pl.ANY)] * len(arrays),
        out_specs=tuple([pl.BlockSpec(memory_space=pl.ANY)] * len(arrays)),
        input_output_aliases={i: i for i in range(len(arrays))},
        compiler_params=pltpu.CompilerParams(vmem_limit_bytes=1024 * 1024),
    )(*arrays)


def gathered(hidden, expert_ids, gate_units, w_gate, w_up, w_down):
    token_count, model_width = hidden.shape
    half_rows = token_count // 2
    tp = lax.axis_index("tp")
    expert_count = lax.axis_size("seq") * lax.axis_size("tp")
    expert = lax.axis_index("seq") * lax.axis_size("tp") + tp
    place = jnp.stack([expert, expert + 1 - 2 * tp, tp]).astype(jnp.int32)

    def z(x, k):
        return lax.ppermute(x, "seq", [(i, i ^ k) for i in range(lax.axis_size("seq"))])

    def diagonal(x):
        flat = [(i, i ^ 3) for i in range(lax.axis_size("seq") * lax.axis_size("ep"))]
        return lax.ppermute(x, ("seq", "ep"), flat)

    def swap(x, axis):
        return lax.ppermute(x, axis, [(0, 1), (1, 0)])

    own = prepare(place, expert_count, hidden, expert_ids, gate_units)
    run = functools.partial(experts, expert_count, place, model_width)
    gate2, up2 = swap(w_gate[0], "tp"), swap(w_up[0], "tp")
    near3, near1, far0, down1, gate1, up1 = hold(
        z(own, 3),
        z(own, 1),
        swap(own, "ep"),
        *stage(own, w_down[0]),
        *stage(own, w_gate[0], w_up[0]),
    )
    held3, gate2, up2 = hold(near3, gate2, up2)
    far3, near2, far2 = swap(near3, "ep"), z(near3, 1), diagonal(held3)
    down2 = swap(down1, "tp")
    weights = gate1, up1, down1, gate2, up2, down2
    near_sum3, far_sum3 = run([near3, far3], weights)
    far_sum3, far0 = hold(far_sum3, far0)
    near2, far2, near_sum3 = hold(near2, far2, near_sum3)
    near_sum2, far_sum2 = run([near2, far2], weights)
    back3, far1, own = hold(swap(far_sum3, "ep"), z(far0, 1), own)
    near_sum0, far_sum0, near_sum1, far_sum1 = run([own, far0, near1, far1], weights)

    def f32(x):
        return x.astype(jnp.float32)

    def bf16(x):
        return x.astype(jnp.bfloat16)

    merged = near_sum3 + f32(back3) + f32(z(bf16(near_sum2), 1)) + f32(diagonal(far_sum2))
    back1, far_sum0 = hold(swap(far_sum1, "ep"), far_sum0)
    here1, there1 = halves(place, jnp.bfloat16, near_sum1, back1)
    seq = [(i, i ^ 1) for i in range(lax.axis_size("seq"))]
    across = [(2 * i + c, 2 * j + 1 - c) for i, j in seq for c in range(2)]
    last_there = lax.ppermute(there1, ("seq", "tp"), across)
    last_here = z(here1, 1)
    here0, there0 = halves(place, jnp.float32, near_sum0, swap(far_sum0, "ep"), z(bf16(merged), 3))
    keep = bf16(here0 + f32(last_here))
    get = bf16(f32(swap(there0, "tp")) + f32(last_there))
    return jnp.where(tp == 0, jnp.concatenate([keep, get]), jnp.concatenate([get, keep]))


def solution(mesh):
    def local(*args):
        token_count = args[0].shape[0]
        seq, ep, tp = (mesh.shape[name] for name in ("seq", "ep", "tp"))
        dense = capacity_of(token_count, seq * tp) * tp >= token_count
        if dense and (seq, ep, tp) == (4, 2, 2):
            return gathered(*args)
        return routed(*args)

    return jax.shard_map(
        local,
        mesh=mesh,
        in_specs=(
            P(("groups", "seq", "ep"), None),
            P(("groups", "seq", "ep"), None),
            P(("groups", "seq", "ep"), None),
            P(("seq", "tp"), None, "ep"),
            P(("seq", "tp"), None, "ep"),
            P(("seq", "tp"), None, "ep"),
        ),
        out_specs=P(("groups", "seq", "ep"), "tp"),
        check_vma=False,
    )
```

```python
import functools

import jax
import jax.numpy as jnp
from jax import lax
from jax.experimental import pallas as pl
from jax.experimental.pallas import tpu as pltpu
from jax.sharding import PartitionSpec as P

TOP = 4


def slice_output(rows_in, gate_cols, up_cols, down_cols):
    gate_pre = jnp.dot(rows_in, gate_cols, preferred_element_type=jnp.float32)
    up_pre = jnp.dot(rows_in, up_cols, preferred_element_type=jnp.float32)
    activation = ((up_pre + 1.0) * gate_pre * jax.nn.sigmoid(1.702 * gate_pre)).astype(jnp.bfloat16)
    return lax.dot_general(
        activation, down_cols, (((1,), (1,)), ((), ())), preferred_element_type=jnp.float32
    ).astype(jnp.bfloat16)


def capacity_of(token_count, expert_count):
    return max(2, (token_count * TOP * 11 + expert_count * 8 - 1) // (expert_count * 8))


def routed(hidden, expert_ids, gate_units, w_gate, w_up, w_down):
    token_count, model_width = hidden.shape
    seq_count = lax.axis_size("seq")
    ep_count = lax.axis_size("ep")
    tp_count = lax.axis_size("tp")
    half_width = model_width // tp_count
    my_half = lax.axis_index("tp")
    expert_count = seq_count * tp_count
    capacity = capacity_of(token_count, expert_count)
    flat_ids = expert_ids.reshape(-1)
    onehot_ids = (flat_ids[:, None] == jnp.arange(expert_count, dtype=jnp.int32)[None, :]).astype(
        jnp.int32
    )
    slot_rank = jnp.sum((jnp.cumsum(onehot_ids, axis=0) - 1) * onehot_ids, axis=1)
    owner_seq = flat_ids // tp_count
    owner_half = flat_ids % tp_count
    send_row = jnp.where(owner_half == my_half, owner_seq * capacity + slot_rank, -1)
    selector = jnp.arange(seq_count * capacity, dtype=jnp.int32)[:, None] == send_row[None, :]
    selector = jnp.any(selector.reshape(seq_count * capacity, token_count, TOP), axis=2).astype(
        jnp.bfloat16
    )
    outgoing = jnp.dot(selector, hidden, preferred_element_type=jnp.float32).astype(jnp.bfloat16)
    outgoing = outgoing.reshape(seq_count, capacity, model_width)
    column_of = (owner_half * seq_count + owner_seq) * capacity + slot_rank
    gate_share = gate_units.reshape(-1).astype(jnp.float32) / 65536.0
    column_ids = jnp.arange(tp_count * seq_count * capacity, dtype=jnp.int32)
    combiner = jnp.where(column_ids[None, :] == column_of[:, None], gate_share[:, None], 0.0)
    combiner = jnp.sum(combiner.reshape(token_count, TOP, -1), axis=1)
    copied = jnp.broadcast_to(outgoing[:, None], (seq_count, ep_count, capacity, model_width))
    copied = copied.reshape(seq_count * ep_count, capacity, model_width)
    arrived = lax.all_to_all(copied, ("seq", "ep"), split_axis=0, concat_axis=0, tiled=True)
    slice_rows = slice_output(arrived.reshape(-1, model_width), w_gate[0], w_up[0], w_down[0])
    slice_rows = slice_rows.reshape(seq_count * ep_count, capacity, model_width)
    came_back = lax.all_to_all(
        lax.all_to_all(slice_rows, ("seq", "ep"), split_axis=0, concat_axis=0, tiled=True),
        "tp",
        split_axis=2,
        concat_axis=0,
        tiled=True,
    )
    came_back = came_back.reshape(tp_count, seq_count, ep_count, capacity, half_width)
    returned = jnp.sum(came_back.astype(jnp.float32), axis=2).astype(jnp.bfloat16)
    result_rows = returned.reshape(-1, half_width).astype(jnp.float32)
    moe_out = jnp.dot(
        combiner, result_rows, precision=lax.Precision.HIGHEST, preferred_element_type=jnp.float32
    )
    return moe_out.astype(jnp.bfloat16)


def expert_kernel(expert_count, count, place_ref, *refs):
    ins, weights = refs[:count], refs[count : count + 6]
    outs, rows = refs[count + 6 : -1], refs[-1]
    model_width = outs[0].shape[1]
    first = 0
    for ref in ins:
        rows[first : first + ref.shape[0], :] = ref[...]
        first += ref.shape[0]
    tail = rows[:, model_width:].astype(jnp.float32)
    lane = lax.broadcasted_iota(jnp.int32, tail.shape, 1)
    x = rows[:, :model_width]
    total = None
    for i in range(2):
        wg, wu, wd = weights[3 * i : 3 * i + 3]
        expert = place_ref[i]
        scale = jnp.where(lane == expert, 256.0, jnp.where(lane == expert + expert_count, 1.0, 0.0))
        weight = jnp.sum(tail * scale, axis=1, keepdims=True) * (1.0 / 65536.0)
        gate_pre = jnp.dot(x, wg[...], preferred_element_type=jnp.float32)
        up_pre = jnp.dot(x, wu[...], preferred_element_type=jnp.float32)
        act = ((up_pre + 1.0) * gate_pre * jax.nn.sigmoid(1.702 * gate_pre)).astype(jnp.bfloat16)
        out = lax.dot_general(
            act, wd[...], (((1,), (1,)), ((), ())), preferred_element_type=jnp.float32
        )
        total = out * weight if total is None else total + out * weight
    half_rows = outs[0].shape[0]
    for i, ref in enumerate(outs):
        ref[...] = total[i * half_rows : (i + 1) * half_rows].astype(ref.dtype)


def experts(expert_count, place, model_width, blocks, weights):
    half_rows, width = blocks[0].shape
    slice_width = weights[0].shape[1]
    vmem = pl.BlockSpec(memory_space=pltpu.VMEM)
    count = len(blocks)
    rows = count * half_rows
    return pl.pallas_call(
        functools.partial(expert_kernel, expert_count, count),
        out_shape=tuple(
            jax.ShapeDtypeStruct((half_rows, model_width), (jnp.float32, jnp.bfloat16)[i % 2])
            for i in range(count)
        ),
        in_specs=[pl.BlockSpec(memory_space=pltpu.SMEM)] + [vmem] * (count + 6),
        out_specs=tuple([vmem] * count),
        scratch_shapes=[pltpu.VMEM((rows, width), jnp.bfloat16)],
        compiler_params=pltpu.CompilerParams(vmem_limit_bytes=20 * 1024 * 1024),
        cost_estimate=pl.CostEstimate(
            flops=2 * rows * model_width * slice_width * 6,
            bytes_accessed=4 * rows * width,
            transcendentals=2 * rows * slice_width,
        ),
    )(place, *blocks, *weights)


def prepare_kernel(place_ref, *refs):
    own, hidden, ids, units, rows, sems = refs[3:]
    copies = [pltpu.make_async_copy(refs[i], refs[i + 4], sems.at[i]) for i in range(3)]
    for copy in copies:
        copy.start()
    model_width, token_count = hidden.shape
    expert_count = (own.shape[1] - model_width) // 2
    half_rows = own.shape[0]
    expert = lax.broadcasted_iota(jnp.int32, (expert_count, token_count), 0)
    shares = jnp.zeros((expert_count, token_count), jnp.int32)
    copies[1].wait()
    copies[2].wait()
    for c in range(ids.shape[0]):
        shares += jnp.where(ids[c : c + 1, :] == expert, units[c : c + 1, :], 0)
    digits = jnp.concatenate([shares // 256, shares % 256], axis=0).astype(jnp.float32)
    rows[:, model_width:] = digits.T.astype(jnp.bfloat16)
    copies[0].wait()
    rows[:, :model_width] = hidden[...].T
    own[...] = rows[pl.ds(pl.multiple_of(place_ref[2] * half_rows, half_rows), half_rows), :]


def prepare(place, expert_count, hidden, expert_ids, gate_units):
    token_count, model_width = hidden.shape
    width = model_width + 2 * expert_count
    arrays = hidden.T, expert_ids.T, gate_units.T
    return pl.pallas_call(
        prepare_kernel,
        out_shape=jax.ShapeDtypeStruct((token_count // 2, width), hidden.dtype),
        in_specs=[pl.BlockSpec(memory_space=pltpu.SMEM)] + [pl.BlockSpec(memory_space=pl.ANY)] * 3,
        out_specs=pl.BlockSpec(memory_space=pltpu.VMEM),
        scratch_shapes=[pltpu.VMEM(x.shape, x.dtype) for x in arrays]
        + [pltpu.VMEM((token_count, width), hidden.dtype), pltpu.SemaphoreType.DMA((3,))],
        compiler_params=pltpu.CompilerParams(vmem_limit_bytes=8 * 1024 * 1024),
    )(place, *[pltpu.with_memory_space_constraint(x, pltpu.HBM) for x in arrays])


def stage_kernel(count, *refs):
    ins, outs, sems = refs[:count], refs[-count - 1 : -1], refs[-1]
    copies = [pltpu.make_async_copy(ins[i], outs[i], sems.at[i]) for i in range(count)]
    for copy in copies:
        copy.start()
    for copy in copies:
        copy.wait()


def stage(after, *arrays):
    return pl.pallas_call(
        functools.partial(stage_kernel, len(arrays)),
        out_shape=tuple(jax.ShapeDtypeStruct(x.shape, x.dtype) for x in arrays),
        in_specs=[pl.BlockSpec(memory_space=pl.ANY)] * (len(arrays) + 1),
        out_specs=tuple([pl.BlockSpec(memory_space=pltpu.VMEM)] * len(arrays)),
        scratch_shapes=[pltpu.SemaphoreType.DMA((len(arrays),))],
        compiler_params=pltpu.CompilerParams(vmem_limit_bytes=8 * 1024 * 1024),
        cost_estimate=pl.CostEstimate(
            flops=0, bytes_accessed=2 * sum(x.size for x in arrays), transcendentals=0
        ),
    )(*[pltpu.with_memory_space_constraint(x, pltpu.HBM) for x in arrays], after)


def halves_kernel(place_ref, *refs):
    ins, (here, there) = refs[:-2], refs[-2:]
    half_width = here.shape[1]
    total = ins[0][...]
    for ref in ins[1:]:
        total = total + ref[...].astype(jnp.float32)
    first = place_ref[2] == 0
    left, right = total[:, :half_width], total[:, half_width:]
    here[...] = jnp.where(first, left, right).astype(here.dtype)
    there[...] = jnp.where(first, right, left).astype(there.dtype)


def halves(place, kept, *arrays):
    rows, width = arrays[0].shape
    vmem = pl.BlockSpec(memory_space=pltpu.VMEM)
    return pl.pallas_call(
        halves_kernel,
        out_shape=tuple(
            jax.ShapeDtypeStruct((rows, width // 2), dtype) for dtype in (kept, jnp.bfloat16)
        ),
        in_specs=[pl.BlockSpec(memory_space=pltpu.SMEM)] + [vmem] * len(arrays),
        out_specs=(vmem, vmem),
        compiler_params=pltpu.CompilerParams(vmem_limit_bytes=8 * 1024 * 1024),
    )(place, *arrays)


def hold_kernel(*refs):
    del refs


def hold(*arrays, weight=0):
    return pl.pallas_call(
        hold_kernel,
        out_shape=tuple(jax.ShapeDtypeStruct(x.shape, x.dtype) for x in arrays),
        in_specs=[pl.BlockSpec(memory_space=pl.ANY)] * len(arrays),
        out_specs=tuple([pl.BlockSpec(memory_space=pl.ANY)] * len(arrays)),
        input_output_aliases={i: i for i in range(len(arrays))},
        compiler_params=pltpu.CompilerParams(vmem_limit_bytes=1024 * 1024),
        cost_estimate=pl.CostEstimate(flops=0, bytes_accessed=weight, transcendentals=0),
    )(*arrays)


def gathered(hidden, expert_ids, gate_units, w_gate, w_up, w_down):
    token_count, model_width = hidden.shape
    half_rows = token_count // 2
    tp = lax.axis_index("tp")
    expert_count = lax.axis_size("seq") * lax.axis_size("tp")
    expert = lax.axis_index("seq") * lax.axis_size("tp") + tp
    place = jnp.stack([expert, expert + 1 - 2 * tp, tp]).astype(jnp.int32)

    def z(x, k):
        return lax.ppermute(x, "seq", [(i, i ^ k) for i in range(lax.axis_size("seq"))])

    def diagonal(x):
        flat = [(i, i ^ 3) for i in range(lax.axis_size("seq") * lax.axis_size("ep"))]
        return lax.ppermute(x, ("seq", "ep"), flat)

    def swap(x, axis):
        return lax.ppermute(x, axis, [(0, 1), (1, 0)])

    own = prepare(place, expert_count, hidden, expert_ids, gate_units)
    run = functools.partial(experts, expert_count, place, model_width)
    gate2, up2 = swap(w_gate[0], "tp"), swap(w_up[0], "tp")
    near3, near1, far0, down1, gate1, up1 = hold(
        z(own, 3),
        z(own, 1),
        swap(own, "ep"),
        *stage(own, w_down[0]),
        *stage(own, w_gate[0], w_up[0]),
    )
    held3, gate2, up2 = hold(near3, gate2, up2)
    far3, near2, far2 = swap(near3, "ep"), z(near3, 1), diagonal(held3)
    down2 = swap(down1, "tp")
    weights = gate1, up1, down1, gate2, up2, down2
    near_sum3, far_sum3 = run([near3, far3], weights)
    far_sum3, far0 = hold(far_sum3, far0)
    near2, far2, near_sum3 = hold(near2, far2, near_sum3)
    near_sum2, far_sum2 = run([near2, far2], weights)
    back3, far1, own = hold(swap(far_sum3, "ep"), z(far0, 1), own)
    near_sum0, far_sum0, near_sum1, far_sum1 = run([own, far0, near1, far1], weights)

    def f32(x):
        return x.astype(jnp.float32)

    def bf16(x):
        return x.astype(jnp.bfloat16)

    merged = near_sum3 + f32(back3) + f32(z(bf16(near_sum2), 1)) + f32(diagonal(far_sum2))
    back1 = swap(far_sum1, "ep")
    here1, there1 = halves(place, jnp.bfloat16, near_sum1, back1)
    seq = [(i, i ^ 1) for i in range(lax.axis_size("seq"))]
    across = [(2 * i + c, 2 * j + 1 - c) for i, j in seq for c in range(2)]
    last_there = lax.ppermute(there1, ("seq", "tp"), across)
    last_here = z(here1, 1)
    here0, there0 = halves(place, jnp.float32, near_sum0, swap(far_sum0, "ep"), z(bf16(merged), 3))
    last_here, last_there = hold(last_here, last_there, weight=1 << 24)
    keep = bf16(here0 + f32(last_here))
    get = bf16(f32(swap(there0, "tp")) + f32(last_there))
    return jnp.where(tp == 0, jnp.concatenate([keep, get]), jnp.concatenate([get, keep]))


def solution(mesh):
    def local(*args):
        token_count = args[0].shape[0]
        seq, ep, tp = (mesh.shape[name] for name in ("seq", "ep", "tp"))
        dense = capacity_of(token_count, seq * tp) * tp >= token_count
        if dense and (seq, ep, tp) == (4, 2, 2):
            return gathered(*args)
        return routed(*args)

    return jax.shard_map(
        local,
        mesh=mesh,
        in_specs=(
            P(("groups", "seq", "ep"), None),
            P(("groups", "seq", "ep"), None),
            P(("groups", "seq", "ep"), None),
            P(("seq", "tp"), None, "ep"),
            P(("seq", "tp"), None, "ep"),
            P(("seq", "tp"), None, "ep"),
        ),
        out_specs=P(("groups", "seq", "ep"), "tp"),
        check_vma=False,
    )
```

```python
import functools

import jax
import jax.numpy as jnp
from jax import lax
from jax.experimental import pallas as pl
from jax.experimental.pallas import tpu as pltpu
from jax.sharding import PartitionSpec as P

TOP = 4


def slice_output(rows_in, gate_cols, up_cols, down_cols):
    gate_pre = jnp.dot(rows_in, gate_cols, preferred_element_type=jnp.float32)
    up_pre = jnp.dot(rows_in, up_cols, preferred_element_type=jnp.float32)
    activation = ((up_pre + 1.0) * gate_pre * jax.nn.sigmoid(1.702 * gate_pre)).astype(jnp.bfloat16)
    return lax.dot_general(
        activation, down_cols, (((1,), (1,)), ((), ())), preferred_element_type=jnp.float32
    ).astype(jnp.bfloat16)


def capacity_of(token_count, expert_count):
    return max(2, (token_count * TOP * 11 + expert_count * 8 - 1) // (expert_count * 8))


def routed(hidden, expert_ids, gate_units, w_gate, w_up, w_down):
    token_count, model_width = hidden.shape
    seq_count = lax.axis_size("seq")
    ep_count = lax.axis_size("ep")
    tp_count = lax.axis_size("tp")
    half_width = model_width // tp_count
    my_half = lax.axis_index("tp")
    expert_count = seq_count * tp_count
    capacity = capacity_of(token_count, expert_count)
    flat_ids = expert_ids.reshape(-1)
    onehot_ids = (flat_ids[:, None] == jnp.arange(expert_count, dtype=jnp.int32)[None, :]).astype(
        jnp.int32
    )
    slot_rank = jnp.sum((jnp.cumsum(onehot_ids, axis=0) - 1) * onehot_ids, axis=1)
    owner_seq = flat_ids // tp_count
    owner_half = flat_ids % tp_count
    send_row = jnp.where(owner_half == my_half, owner_seq * capacity + slot_rank, -1)
    selector = jnp.arange(seq_count * capacity, dtype=jnp.int32)[:, None] == send_row[None, :]
    selector = jnp.any(selector.reshape(seq_count * capacity, token_count, TOP), axis=2).astype(
        jnp.bfloat16
    )
    outgoing = jnp.dot(selector, hidden, preferred_element_type=jnp.float32).astype(jnp.bfloat16)
    outgoing = outgoing.reshape(seq_count, capacity, model_width)
    column_of = (owner_half * seq_count + owner_seq) * capacity + slot_rank
    gate_share = gate_units.reshape(-1).astype(jnp.float32) / 65536.0
    column_ids = jnp.arange(tp_count * seq_count * capacity, dtype=jnp.int32)
    combiner = jnp.where(column_ids[None, :] == column_of[:, None], gate_share[:, None], 0.0)
    combiner = jnp.sum(combiner.reshape(token_count, TOP, -1), axis=1)
    copied = jnp.broadcast_to(outgoing[:, None], (seq_count, ep_count, capacity, model_width))
    copied = copied.reshape(seq_count * ep_count, capacity, model_width)
    arrived = lax.all_to_all(copied, ("seq", "ep"), split_axis=0, concat_axis=0, tiled=True)
    slice_rows = slice_output(arrived.reshape(-1, model_width), w_gate[0], w_up[0], w_down[0])
    slice_rows = slice_rows.reshape(seq_count * ep_count, capacity, model_width)
    came_back = lax.all_to_all(
        lax.all_to_all(slice_rows, ("seq", "ep"), split_axis=0, concat_axis=0, tiled=True),
        "tp",
        split_axis=2,
        concat_axis=0,
        tiled=True,
    )
    came_back = came_back.reshape(tp_count, seq_count, ep_count, capacity, half_width)
    returned = jnp.sum(came_back.astype(jnp.float32), axis=2).astype(jnp.bfloat16)
    result_rows = returned.reshape(-1, half_width).astype(jnp.float32)
    moe_out = jnp.dot(
        combiner, result_rows, precision=lax.Precision.HIGHEST, preferred_element_type=jnp.float32
    )
    return moe_out.astype(jnp.bfloat16)


def expert_kernel(expert_count, count, place_ref, *refs):
    ins, weights = refs[:count], refs[count : count + 6]
    outs, rows = refs[count + 6 : -1], refs[-1]
    model_width = outs[0].shape[1]
    first = 0
    for ref in ins:
        rows[first : first + ref.shape[0], :] = ref[...]
        first += ref.shape[0]
    tail = rows[:, model_width:].astype(jnp.float32)
    lane = lax.broadcasted_iota(jnp.int32, tail.shape, 1)
    x = rows[:, :model_width]
    total = None
    for i in range(2):
        wg, wu, wd = weights[3 * i : 3 * i + 3]
        expert = place_ref[i]
        scale = jnp.where(lane == expert, 256.0, jnp.where(lane == expert + expert_count, 1.0, 0.0))
        weight = jnp.sum(tail * scale, axis=1, keepdims=True) * (1.0 / 65536.0)
        gate_pre = jnp.dot(x, wg[...], preferred_element_type=jnp.float32)
        up_pre = jnp.dot(x, wu[...], preferred_element_type=jnp.float32)
        act = ((up_pre + 1.0) * gate_pre * jax.nn.sigmoid(1.702 * gate_pre)).astype(jnp.bfloat16)
        out = jnp.dot(act, wd[...], preferred_element_type=jnp.float32)
        total = out * weight if total is None else total + out * weight
    half_rows = outs[0].shape[0]
    for i, ref in enumerate(outs):
        ref[...] = total[i * half_rows : (i + 1) * half_rows].astype(ref.dtype)


def experts(expert_count, place, model_width, blocks, weights):
    half_rows, width = blocks[0].shape
    slice_width = weights[0].shape[1]
    vmem = pl.BlockSpec(memory_space=pltpu.VMEM)
    count = len(blocks)
    rows = count * half_rows
    return pl.pallas_call(
        functools.partial(expert_kernel, expert_count, count),
        out_shape=tuple(
            jax.ShapeDtypeStruct((half_rows, model_width), (jnp.float32, jnp.bfloat16)[i % 2])
            for i in range(count)
        ),
        in_specs=[pl.BlockSpec(memory_space=pltpu.SMEM)] + [vmem] * (count + 6),
        out_specs=tuple([vmem] * count),
        scratch_shapes=[pltpu.VMEM((rows, width), jnp.bfloat16)],
        compiler_params=pltpu.CompilerParams(vmem_limit_bytes=20 * 1024 * 1024),
        cost_estimate=pl.CostEstimate(
            flops=2 * rows * model_width * slice_width * 6,
            bytes_accessed=4 * rows * width,
            transcendentals=2 * rows * slice_width,
        ),
    )(place, *blocks, *weights)


def prepare_kernel(place_ref, *refs):
    own, hidden, ids, units, rows, sems = refs[3:]
    copies = [pltpu.make_async_copy(refs[i], refs[i + 4], sems.at[i]) for i in range(3)]
    for copy in copies:
        copy.start()
    model_width, token_count = hidden.shape
    expert_count = (own.shape[1] - model_width) // 2
    half_rows = own.shape[0]
    expert = lax.broadcasted_iota(jnp.int32, (expert_count, token_count), 0)
    shares = jnp.zeros((expert_count, token_count), jnp.int32)
    copies[1].wait()
    copies[2].wait()
    for c in range(ids.shape[0]):
        shares += jnp.where(ids[c : c + 1, :] == expert, units[c : c + 1, :], 0)
    digits = jnp.concatenate([shares // 256, shares % 256], axis=0).astype(jnp.float32)
    rows[:, model_width:] = digits.T.astype(jnp.bfloat16)
    copies[0].wait()
    rows[:, :model_width] = hidden[...].T
    own[...] = rows[pl.ds(pl.multiple_of(place_ref[2] * half_rows, half_rows), half_rows), :]


def prepare(place, expert_count, hidden, expert_ids, gate_units):
    token_count, model_width = hidden.shape
    width = model_width + 2 * expert_count
    arrays = hidden.T, expert_ids.T, gate_units.T
    return pl.pallas_call(
        prepare_kernel,
        out_shape=jax.ShapeDtypeStruct((token_count // 2, width), hidden.dtype),
        in_specs=[pl.BlockSpec(memory_space=pltpu.SMEM)] + [pl.BlockSpec(memory_space=pl.ANY)] * 3,
        out_specs=pl.BlockSpec(memory_space=pltpu.VMEM),
        scratch_shapes=[pltpu.VMEM(x.shape, x.dtype) for x in arrays]
        + [pltpu.VMEM((token_count, width), hidden.dtype), pltpu.SemaphoreType.DMA((3,))],
        compiler_params=pltpu.CompilerParams(vmem_limit_bytes=8 * 1024 * 1024),
    )(place, *[pltpu.with_memory_space_constraint(x, pltpu.HBM) for x in arrays])


def stage_kernel(count, *refs):
    ins, outs, sems = refs[:count], refs[-count - 1 : -1], refs[-1]
    copies = [pltpu.make_async_copy(ins[i], outs[i], sems.at[i]) for i in range(count)]
    for copy in copies:
        copy.start()
    for copy in copies:
        copy.wait()


def stage(after, *arrays):
    return pl.pallas_call(
        functools.partial(stage_kernel, len(arrays)),
        out_shape=tuple(jax.ShapeDtypeStruct(x.shape, x.dtype) for x in arrays),
        in_specs=[pl.BlockSpec(memory_space=pl.ANY)] * (len(arrays) + 1),
        out_specs=tuple([pl.BlockSpec(memory_space=pltpu.VMEM)] * len(arrays)),
        scratch_shapes=[pltpu.SemaphoreType.DMA((len(arrays),))],
        compiler_params=pltpu.CompilerParams(vmem_limit_bytes=8 * 1024 * 1024),
        cost_estimate=pl.CostEstimate(
            flops=0, bytes_accessed=2 * sum(x.size for x in arrays), transcendentals=0
        ),
    )(*[pltpu.with_memory_space_constraint(x, pltpu.HBM) for x in arrays], after)


def halves_kernel(place_ref, *refs):
    ins, (here, there) = refs[:-2], refs[-2:]
    half_width = here.shape[1]
    total = ins[0][...]
    for ref in ins[1:]:
        total = total + ref[...].astype(jnp.float32)
    first = place_ref[2] == 0
    left, right = total[:, :half_width], total[:, half_width:]
    here[...] = jnp.where(first, left, right).astype(here.dtype)
    there[...] = jnp.where(first, right, left).astype(there.dtype)


def halves(place, kept, *arrays):
    rows, width = arrays[0].shape
    vmem = pl.BlockSpec(memory_space=pltpu.VMEM)
    return pl.pallas_call(
        halves_kernel,
        out_shape=tuple(
            jax.ShapeDtypeStruct((rows, width // 2), dtype) for dtype in (kept, jnp.bfloat16)
        ),
        in_specs=[pl.BlockSpec(memory_space=pltpu.SMEM)] + [vmem] * len(arrays),
        out_specs=(vmem, vmem),
        compiler_params=pltpu.CompilerParams(vmem_limit_bytes=8 * 1024 * 1024),
    )(place, *arrays)


def turn_kernel(w, after_ref, out, held, sem):
    del after_ref
    copy = pltpu.make_async_copy(w, held, sem)
    copy.start()
    copy.wait()
    out[...] = held[...].T


def turned(after, w):
    return pl.pallas_call(
        turn_kernel,
        out_shape=jax.ShapeDtypeStruct(w.shape[::-1], w.dtype),
        in_specs=[pl.BlockSpec(memory_space=pl.ANY)] * 2,
        out_specs=pl.BlockSpec(memory_space=pltpu.VMEM),
        scratch_shapes=[pltpu.VMEM(w.shape, w.dtype), pltpu.SemaphoreType.DMA],
        compiler_params=pltpu.CompilerParams(vmem_limit_bytes=8 * 1024 * 1024),
        cost_estimate=pl.CostEstimate(flops=0, bytes_accessed=2 * w.size, transcendentals=0),
    )(pltpu.with_memory_space_constraint(w, pltpu.HBM), after)


def hold_kernel(*refs):
    del refs


def hold(*arrays, weight=0):
    return pl.pallas_call(
        hold_kernel,
        out_shape=tuple(jax.ShapeDtypeStruct(x.shape, x.dtype) for x in arrays),
        in_specs=[pl.BlockSpec(memory_space=pl.ANY)] * len(arrays),
        out_specs=tuple([pl.BlockSpec(memory_space=pl.ANY)] * len(arrays)),
        input_output_aliases={i: i for i in range(len(arrays))},
        compiler_params=pltpu.CompilerParams(vmem_limit_bytes=1024 * 1024),
        cost_estimate=pl.CostEstimate(flops=0, bytes_accessed=weight, transcendentals=0),
    )(*arrays)


def gathered(hidden, expert_ids, gate_units, w_gate, w_up, w_down):
    token_count, model_width = hidden.shape
    half_rows = token_count // 2
    tp = lax.axis_index("tp")
    expert_count = lax.axis_size("seq") * lax.axis_size("tp")
    expert = lax.axis_index("seq") * lax.axis_size("tp") + tp
    place = jnp.stack([expert, expert + 1 - 2 * tp, tp]).astype(jnp.int32)

    def z(x, k):
        return lax.ppermute(x, "seq", [(i, i ^ k) for i in range(lax.axis_size("seq"))])

    def diagonal(x):
        flat = [(i, i ^ 3) for i in range(lax.axis_size("seq") * lax.axis_size("ep"))]
        return lax.ppermute(x, ("seq", "ep"), flat)

    def swap(x, axis):
        return lax.ppermute(x, axis, [(0, 1), (1, 0)])

    own = prepare(place, expert_count, hidden, expert_ids, gate_units)
    run = functools.partial(experts, expert_count, place, model_width)
    gate2, up2 = swap(w_gate[0], "tp"), swap(w_up[0], "tp")
    near3, near1, far0, down1, gate1, up1 = hold(
        z(own, 3),
        z(own, 1),
        swap(own, "ep"),
        turned(own, w_down[0]),
        *stage(own, w_gate[0], w_up[0]),
    )
    held3, gate2, up2 = hold(near3, gate2, up2)
    far3, near2, far2 = swap(near3, "ep"), z(near3, 1), diagonal(held3)
    down2 = swap(down1, "tp")
    weights = gate1, up1, down1, gate2, up2, down2
    near_sum3, far_sum3 = run([near3, far3], weights)
    far_sum3, far0 = hold(far_sum3, far0)
    near2, far2, near_sum3 = hold(near2, far2, near_sum3)
    near_sum2, far_sum2 = run([near2, far2], weights)
    back3, far1, own = hold(swap(far_sum3, "ep"), z(far0, 1), own)
    near_sum0, far_sum0, near_sum1, far_sum1 = run([own, far0, near1, far1], weights)

    def f32(x):
        return x.astype(jnp.float32)

    def bf16(x):
        return x.astype(jnp.bfloat16)

    merged = near_sum3 + f32(back3) + f32(z(bf16(near_sum2), 1)) + f32(diagonal(far_sum2))
    back1 = swap(far_sum1, "ep")
    here1, there1 = halves(place, jnp.bfloat16, near_sum1, back1)
    seq = [(i, i ^ 1) for i in range(lax.axis_size("seq"))]
    across = [(2 * i + c, 2 * j + 1 - c) for i, j in seq for c in range(2)]
    last_there = lax.ppermute(there1, ("seq", "tp"), across)
    last_here = z(here1, 1)
    here0, there0 = halves(place, jnp.float32, near_sum0, swap(far_sum0, "ep"), z(bf16(merged), 3))
    last_here, last_there = hold(last_here, last_there, weight=1 << 24)
    keep = bf16(here0 + f32(last_here))
    get = bf16(f32(swap(there0, "tp")) + f32(last_there))
    return jnp.where(tp == 0, jnp.concatenate([keep, get]), jnp.concatenate([get, keep]))


def solution(mesh):
    def local(*args):
        token_count = args[0].shape[0]
        seq, ep, tp = (mesh.shape[name] for name in ("seq", "ep", "tp"))
        dense = capacity_of(token_count, seq * tp) * tp >= token_count
        if dense and (seq, ep, tp) == (4, 2, 2):
            return gathered(*args)
        return routed(*args)

    return jax.shard_map(
        local,
        mesh=mesh,
        in_specs=(
            P(("groups", "seq", "ep"), None),
            P(("groups", "seq", "ep"), None),
            P(("groups", "seq", "ep"), None),
            P(("seq", "tp"), None, "ep"),
            P(("seq", "tp"), None, "ep"),
            P(("seq", "tp"), None, "ep"),
        ),
        out_specs=P(("groups", "seq", "ep"), "tp"),
        check_vma=False,
    )
```
